768 devices in a mesh: blk: 32 (over y_lo, x, core), grp: 24 (over y_hi, z).
Axes of the slice: x: 4, y: 8 (y_hi: 2, y_lo: 4; y = y_hi * 4 + y_lo), z: 12, core: 2. Of those that a mesh axis runs over, the one named last changes fastest.
Arguments:
- images: bfloat16 [18432, 1152], P('blk'), may hold values from -0.5 to 0.5, as said below
- texts: bfloat16 [18432, 1152], P(('blk', 'grp')), may hold values from -0.5 to 0.5
- log_scale: float32 [1], replicated, may hold values from 1.6 to 2.3
- bias: float32 [1], replicated, may hold values from -3 to -1
Outputs:
- d_images: float32 [18432, 1152], P(('blk', 'grp'))
- d_texts: float32 [18432, 1152], P(('blk', 'grp'))
The draws below stay inside these ranges and needn't reach their ends.
Inputs may be any that keep to these rules, and one draw needn't show every extreme that they name: `images`: rows of image embeddings.
All inputs are finite; a program needn't handle non-finite values.
Results may differ from the reference program's by a relative error of at most 0.0051.
Values may be sent and summed in bfloat16 or wider, within the bound.
No kernel may reach another device: no remote copies, remote signals or barrier semaphores. Data moves between devices by JAX's collectives and lax.ppermute only.
A program may use at most 32 MiB of HBM per device.

```python
import math
import jax
import jax.numpy as jnp
from jax import lax

E = 1152
TXT_DEV = 24
PAIRS = 18432
N_BLK = 32
N_GRP = 24


def row_scales(key):
    return jnp.exp(jax.random.uniform(key, (PAIRS, 1), jnp.float32, math.log(0.3), math.log(3.0)))


def normal_rows(key):
    first, second = jax.random.split(key)
    base = jnp.clip(jax.random.normal(first, (PAIRS, E), jnp.float32), -5.0, 5.0)
    return (base * row_scales(second) * 0.03).astype(jnp.bfloat16)


def draw_images(key, part):
    key = jax.random.fold_in(key, 11)
    return normal_rows(key)


def draw_texts(key, part):
    key = jax.random.fold_in(key, 23)
    return normal_rows(key)


def setup_inputs(seed: int = 0) -> dict:
    key_list = jax.random.split(jax.random.key(seed), 5)
    images = draw_images(jax.random.fold_in(key_list[4], 71), 0)
    texts = draw_texts(jax.random.fold_in(key_list[4], 71), 0)
    log_scale = jnp.clip(jax.random.uniform(key_list[2], (1,), jnp.float32, 1.6, 2.3), 1.6, 2.3)
    bias = jnp.clip(jax.random.uniform(key_list[3], (1,), jnp.float32, -3.0, -1.0), -3.0, -1.0)
    return dict(images=images, texts=texts, log_scale=log_scale, bias=bias)


def normalize(vectors):
    values = vectors.astype(jnp.float32)
    inverse = lax.rsqrt(lax.optimization_barrier(jnp.sum(values * values, axis=1, keepdims=True)) + 1e-06)
    return (values * inverse, inverse)

def unnormalize(unit_rows, inverse, grad_rows):
    inner = lax.optimization_barrier(jnp.sum(unit_rows * grad_rows, axis=1, keepdims=True))
    return inverse * (grad_rows - unit_rows * inner)

def reference(images, texts, log_scale, bias):
    logit_scale = jnp.exp(log_scale[0])
    logit_shift = bias[0]
    unit_x, inv_x = normalize(images)
    unit_y, inv_y = normalize(texts)
    image_unit = unit_x.astype(jnp.bfloat16)
    text_unit = unit_y.astype(jnp.bfloat16)
    block_rows = TXT_DEV * N_GRP
    col_ids = jnp.arange(PAIRS, dtype=jnp.int32)

    def step(text_total, block_id):
        image_block = lax.dynamic_slice_in_dim(image_unit, block_id * block_rows, block_rows, 0)
        logits = jnp.dot(image_block, text_unit.T, preferred_element_type=jnp.float32) * logit_scale + logit_shift
        row_ids = block_id * block_rows + jnp.arange(block_rows, dtype=jnp.int32)
        positive = (row_ids[:, None] == col_ids[None, :]).astype(jnp.float32)
        weights = (jax.nn.sigmoid(logits) - positive).astype(jnp.bfloat16)
        grad_block = jnp.dot(weights, text_unit, preferred_element_type=jnp.float32) * logit_scale
        text_total = text_total + jnp.dot(weights.T, image_block, preferred_element_type=jnp.float32) * logit_scale
        return (text_total, grad_block)
    text_total, grad_blocks = lax.scan(step, jnp.zeros((PAIRS, E), jnp.float32), jnp.arange(N_BLK, dtype=jnp.int32))
    grad_x = grad_blocks.reshape(PAIRS, E)
    d_images = unnormalize(unit_x, inv_x, grad_x)
    d_texts = unnormalize(unit_y, inv_y, text_total)
    return (d_images, d_texts)
```

```python
import jax
import jax.numpy as jnp
from jax import lax
from jax.sharding import Mesh, PartitionSpec as P

SIZES = (4, 4, 2, 2, 3, 2, 2)
NAMES = ("yl", "x", "c", "yh", "z3", "z2", "z1")
ROWS = 24
BF = jnp.bfloat16
F32 = jnp.float32
TEXT_SIDE = "perm"
GATHER = "direct"


def normalize(vectors):
    values = vectors.astype(F32)
    inverse = lax.rsqrt(jnp.sum(values * values, axis=1, keepdims=True) + 1e-06)
    return values * inverse, inverse


def unnormalize(unit_rows, inverse, grad_rows):
    inner = jnp.sum(unit_rows * grad_rows, axis=1, keepdims=True)
    return inverse * (grad_rows - unit_rows * inner)


def pair_perm(size, distance):
    perm = []
    for core in range(2):
        for at in range(size):
            step = distance if (at // distance) % 2 == 0 else -distance
            if core:
                step = -step
            perm.append((core * size + at, core * size + (at + step) % size))
    return perm


def swap(value, axis):
    return lax.ppermute(value, axis, [(0, 1), (1, 0)])


def pick(value, axis, index):
    return lax.dynamic_index_in_dim(value, index, axis, keepdims=False)


def gather(texts):
    if GATHER == "direct":
        copies = jnp.broadcast_to(texts[None], (16, *texts.shape))
        own = lax.all_to_all(copies, ("yl", "x"), 0, 0).reshape(-1, texts.shape[1])
    else:
        copies = jnp.broadcast_to(texts[None], (4, *texts.shape))
        part = lax.all_to_all(copies, "yl", 0, 0).reshape(1, -1, texts.shape[1])
        part = jnp.broadcast_to(part, (4, *part.shape[1:]))
        own = lax.all_to_all(part, "x", 0, 0)
        own = own.reshape(4, 4, 24, -1).swapaxes(0, 1).reshape(-1, texts.shape[1])
    return own


def local(images, texts, log_scale, bias):
    width = texts.shape[1]
    scale = jnp.exp(log_scale[0])
    z1 = lax.axis_index("z1")
    group = lax.axis_index(("yh", "z3", "z2", "z1"))
    blocks = images.reshape(12, 2, ROWS, width)
    mine, theirs = pick(blocks, 1, z1), pick(blocks, 1, 1 - z1)
    image_rows = jnp.concatenate([theirs, mine], 0).reshape(-1, width)
    own = gather(texts)
    other = swap(own, "c")
    text_rows = jnp.concatenate([own, other], 0)
    xn = normalize(image_rows)[0].astype(BF)
    yn = normalize(text_rows)[0].astype(BF)
    logits = jnp.dot(xn, yn.T, preferred_element_type=F32) * scale + bias[0]
    w = jax.nn.sigmoid(logits).astype(BF)
    half = xn.shape[0] // 2
    gx_send = jnp.dot(w[:half], yn, preferred_element_type=F32).astype(BF)
    gx_got = lax.ppermute(gx_send, ("c", "z3", "z2", "z1"), pair_perm(12, 1))
    gy = jnp.einsum("ic,ie->ce", w, xn, preferred_element_type=F32)
    n_own = own.shape[0]
    gy_got = swap(gy[n_own:].astype(BF), "c")
    gx_keep = jnp.dot(w[half:], yn, preferred_element_type=F32)
    gx = (gx_keep + gx_got.astype(F32)).astype(BF).reshape(12, ROWS, width)
    gy = gy[:n_own] + gy_got.astype(F32)
    gx = lax.all_to_all(gx, ("yh", "z3", "z2"), 0, 0)
    if TEXT_SIDE == "a2a":
        gy = gy.astype(BF).reshape(16, ROWS, width)
        gy = lax.all_to_all(gy, ("yl", "x"), 0, 0)
        gy = jnp.sum(gy.astype(F32), 0)
    else:
        x, yl = lax.axis_index("x"), lax.axis_index("yl")
        gy = gy.reshape(2, 2, 2, 2, ROWS, width)
        def stage(gy, axis, bit, move):
            keep = pick(gy, axis, bit)
            send = pick(gy, axis, 1 - bit).astype(BF)
            return keep + move(send).astype(F32)
        flip = lambda n, d: [(i, i ^ d) for i in range(n)]
        gy = stage(gy, 3, x % 2, lambda v: lax.ppermute(v, ("x", "c"), [((i * 2 + c), ((i + (1 if (i + c) % 2 == 0 else -1)) % 4) * 2 + c) for i in range(4) for c in range(2)]))
        gy = stage(gy, 2, x // 2, lambda v: lax.ppermute(v, "x", flip(4, 2)))
        gy = stage(gy, 1, yl % 2, lambda v: lax.ppermute(v, "yl", flip(4, 1)))
        gy = stage(gy, 0, yl // 2, lambda v: lax.ppermute(v, "yl", flip(4, 2)))
    gx = jnp.sum(gx.astype(F32), 0)
    own_images = lax.dynamic_slice_in_dim(images, group * ROWS, ROWS, 0)
    unit_x, inv_x = normalize(own_images)
    unit_y, inv_y = normalize(texts)
    gx = (gx - unit_y.astype(BF).astype(F32)) * scale
    gy = (gy - unit_x.astype(BF).astype(F32)) * scale
    return unnormalize(unit_x, inv_x, gx), unnormalize(unit_y, inv_y, gy)


def solution(mesh):
    fine = Mesh(mesh.devices.reshape(SIZES), NAMES)
    blk, grp = NAMES[:3], NAMES[3:]
    return jax.shard_map(
        local,
        mesh=fine,
        in_specs=(P(blk, None), P(blk + grp, None), P(), P()),
        out_specs=(P(blk + grp, None), P(blk + grp, None)),
        check_vma=False,
    )
```

```python
import jax
import jax.numpy as jnp
from jax import lax
from jax.sharding import Mesh, PartitionSpec as P

SIZES = (4, 4, 2, 2, 3, 2, 2)
NAMES = ("yl", "x", "c", "yh", "z3", "z2", "z1")
ROWS = 24
BF = jnp.bfloat16
F32 = jnp.float32


def normalize(vectors):
    values = vectors.astype(F32)
    inverse = lax.rsqrt(jnp.sum(values * values, axis=1, keepdims=True) + 1e-06)
    return values * inverse, inverse


def unnormalize(unit_rows, inverse, grad_rows):
    inner = jnp.sum(unit_rows * grad_rows, axis=1, keepdims=True)
    return inverse * (grad_rows - unit_rows * inner)


def pair_perm(size, distance):
    perm = []
    for core in range(2):
        for at in range(size):
            step = distance if (at // distance) % 2 == 0 else -distance
            if core:
                step = -step
            perm.append((core * size + at, core * size + (at + step) % size))
    return perm


def flip(value, axis, distance):
    size = lax.axis_size(axis)
    return lax.ppermute(value, axis, [(i, i ^ distance) for i in range(size)])


def pick(value, axis, index):
    return lax.dynamic_index_in_dim(value, index, axis, keepdims=False)


PLANE = ("yl", "x", "c", "yh")


def member(core, window, pos, x):
    y = (4 * window + pos - 2 * core) % 8
    return ((y % 4 * 4 + x) * 2 + core) * 2 + y // 4


PLACES = [(c, w, p, x) for c in range(2) for w in range(2) for p in range(4) for x in range(4)]


def gather(texts):
    groups = [
        [member(c, w, p, x) for x in range(4) for p in range(4)] for c in range(2) for w in range(2)
    ]
    copies = jnp.broadcast_to(texts[None], (16, *texts.shape))
    own = lax.all_to_all(copies, PLANE, 0, 0, axis_index_groups=groups)
    return own.reshape(-1, texts.shape[1])


def scatter_sum(total):
    pos = (lax.axis_index("yl") + 2 * lax.axis_index("c")) % 4
    for at, dp, dx in ((lax.axis_index("x"), 0, 1), (pos, 1, 0)):
        got = [
            lax.ppermute(
                pick(total, 0, at ^ d).astype(BF),
                PLANE,
                [(member(*m), member(m[0], m[1], m[2] ^ d * dp, m[3] ^ d * dx)) for m in PLACES],
            )
            for d in (1, 2, 3)
        ]
        total = pick(total, 0, at) + got[0].astype(F32) + got[1].astype(F32) + got[2].astype(F32)
    return total


def local(images, texts, log_scale, bias):
    width = texts.shape[1]
    scale = jnp.exp(log_scale[0])
    z1 = lax.axis_index("z1")
    group = lax.axis_index(("yh", "z3", "z2", "z1"))
    blocks = images.reshape(6, 2, 2, ROWS, width)
    mine, theirs = (pick(blocks, 2, i).swapaxes(0, 1).reshape(12, ROWS, width) for i in (z1, 1 - z1))
    image_rows = jnp.concatenate([theirs, mine], 0).reshape(-1, width)
    own = gather(texts)
    other = flip(own, "c", 1)
    text_rows = jnp.concatenate([own, other], 0)
    xn = normalize(image_rows)[0].astype(BF)
    yn = normalize(text_rows)[0].astype(BF)
    logits = jnp.dot(xn, yn.T, preferred_element_type=F32) * scale + bias[0]
    w = jax.nn.sigmoid(logits).astype(BF)
    half = xn.shape[0] // 2
    n_own = own.shape[0]
    gx_send = jnp.dot(w[:half], yn, preferred_element_type=F32).astype(BF)
    w, gx_send = lax.optimization_barrier((w, gx_send))
    gx_got = lax.ppermute(gx_send, ("c", "z3", "z2", "z1"), pair_perm(12, 1))
    gy_other = jnp.einsum("ic,ie->ce", w[:, n_own:], xn, preferred_element_type=F32).astype(BF)
    gy_own = jnp.einsum("ic,ie->ce", w[:, :n_own], xn, preferred_element_type=F32)
    gy_got = flip(gy_other, "c", 1)
    gx_keep = jnp.dot(w[half:], yn, preferred_element_type=F32)
    gx_got, gx_keep = lax.optimization_barrier((gx_got, gx_keep))
    z2 = lax.axis_index("z2")
    gx = (gx_keep + gx_got.astype(F32)).reshape(2, 6, ROWS, width)
    gx_got = lax.ppermute(pick(gx, 0, 1 - z2).astype(BF), ("c", "z3", "z2", "z1"), pair_perm(12, 2))
    gx = (pick(gx, 0, z2) + gx_got.astype(F32)).astype(BF)
    gx = lax.all_to_all(gx, ("yh", "z3"), 0, 0)
    gy = (gy_own + gy_got.astype(F32)).reshape(4, 4, ROWS, width)
    gy = scatter_sum(gy)
    gx = jnp.sum(gx.astype(F32), 0)
    own_images = lax.dynamic_slice_in_dim(images, group * ROWS, ROWS, 0)
    unit_x, inv_x = normalize(own_images)
    unit_y, inv_y = normalize(texts)
    gx = (gx - unit_y.astype(BF).astype(F32)) * scale
    gy = (gy - unit_x.astype(BF).astype(F32)) * scale
    return unnormalize(unit_x, inv_x, gx), unnormalize(unit_y, inv_y, gy)


def solution(mesh):
    fine = Mesh(mesh.devices.reshape(SIZES), NAMES)
    blk, grp = NAMES[:3], NAMES[3:]
    return jax.shard_map(
        local,
        mesh=fine,
        in_specs=(P(blk, None), P(blk + grp, None), P(), P()),
        out_specs=(P(blk + grp, None), P(blk + grp, None)),
        check_vma=False,
    )
```

```python
import jax
import jax.numpy as jnp
from jax import lax
from jax.sharding import Mesh, PartitionSpec as P

SIZES = (4, 4, 2, 2, 3, 2, 2)
NAMES = ("yl", "x", "c", "yh", "z3", "z2", "z1")
ROWS = 24
BF = jnp.bfloat16
F32 = jnp.float32


def normalize(vectors):
    values = vectors.astype(F32)
    inverse = lax.rsqrt(jnp.sum(values * values, axis=1, keepdims=True) + 1e-06)
    return values * inverse, inverse


def unnormalize(unit_rows, inverse, grad_rows):
    inner = jnp.sum(unit_rows * grad_rows, axis=1, keepdims=True)
    return inverse * (grad_rows - unit_rows * inner)


def pair_perm(size, distance):
    perm = []
    for core in range(2):
        for at in range(size):
            step = distance if (at // distance) % 2 == 0 else -distance
            if core:
                step = -step
            perm.append((core * size + at, core * size + (at + step) % size))
    return perm


def flip(value, axis, distance):
    size = lax.axis_size(axis)
    return lax.ppermute(value, axis, [(i, i ^ distance) for i in range(size)])


def pick(value, axis, index):
    return lax.dynamic_index_in_dim(value, index, axis, keepdims=False)


PLANE = ("yl", "x", "c", "yh")


def member(core, window, pos, x):
    y = (4 * window + pos - 2 * core) % 8
    return ((y % 4 * 4 + x) * 2 + core) * 2 + y // 4


PLACES = [(c, w, p, x) for c in range(2) for w in range(2) for p in range(4) for x in range(4)]


def gather(texts):
    groups = [
        [member(c, w, p, x) for x in range(4) for p in range(4)] for c in range(2) for w in range(2)
    ]
    copies = jnp.broadcast_to(texts[None], (16, *texts.shape))
    own = lax.all_to_all(copies, PLANE, 0, 0, axis_index_groups=groups)
    return own.reshape(-1, texts.shape[1])


def scatter_sum(total):
    pos = (lax.axis_index("yl") + 2 * lax.axis_index("c")) % 4
    for at, dp, dx in ((lax.axis_index("x"), 0, 1), (pos, 1, 0)):
        got = [
            lax.ppermute(
                pick(total, 0, at ^ d).astype(BF),
                PLANE,
                [(member(*m), member(m[0], m[1], m[2] ^ d * dp, m[3] ^ d * dx)) for m in PLACES],
            )
            for d in (1, 2, 3)
        ]
        total = pick(total, 0, at) + got[0].astype(F32) + got[1].astype(F32) + got[2].astype(F32)
    return total


def local(images, texts, log_scale, bias):
    width = texts.shape[1]
    scale = jnp.exp(log_scale[0])
    z1 = lax.axis_index("z1")
    group = lax.axis_index(("yh", "z3", "z2", "z1"))
    blocks = images.reshape(6, 2, 2, ROWS, width)
    mine, theirs = (pick(blocks, 2, i).swapaxes(0, 1).reshape(12, ROWS, width) for i in (z1, 1 - z1))
    image_rows = jnp.concatenate([theirs, mine], 0).reshape(-1, width)
    own = gather(texts)
    other = flip(own, "c", 1)
    text_rows = jnp.concatenate([own, other], 0)
    xn = normalize(image_rows)[0].astype(BF)
    yn = lax.optimization_barrier(normalize(text_rows)[0].astype(BF))
    logits = jnp.dot(xn, yn.T, preferred_element_type=F32) * scale + bias[0]
    w = jax.nn.sigmoid(logits).astype(BF)
    half = xn.shape[0] // 2
    n_own = own.shape[0]
    gx_send = jnp.dot(w[:half], yn, preferred_element_type=F32).astype(BF)
    w, gx_send = lax.optimization_barrier((w, gx_send))
    gx_got = lax.ppermute(gx_send, ("c", "z3", "z2", "z1"), pair_perm(12, 1))
    gy_other = jnp.einsum("ic,ie->ce", w[:, n_own:], xn, preferred_element_type=F32).astype(BF)
    gy_own = jnp.einsum("ic,ie->ce", w[:, :n_own], xn, preferred_element_type=F32)
    gy_got = flip(gy_other, "c", 1)
    gx_keep = jnp.dot(w[half:], yn, preferred_element_type=F32)
    gx_got, gx_keep = lax.optimization_barrier((gx_got, gx_keep))
    z2 = lax.axis_index("z2")
    gx = (gx_keep + gx_got.astype(F32)).reshape(2, 6, ROWS, width)
    gx_got = lax.ppermute(pick(gx, 0, 1 - z2).astype(BF), ("c", "z3", "z2", "z1"), pair_perm(12, 2))
    gx = (pick(gx, 0, z2) + gx_got.astype(F32)).astype(BF)
    gx = lax.all_to_all(gx, ("yh", "z3"), 0, 0)
    gy = (gy_own + gy_got.astype(F32)).reshape(4, 4, ROWS, width)
    gy = scatter_sum(gy)
    gx = jnp.sum(gx.astype(F32), 0)
    own_images = lax.dynamic_slice_in_dim(images, group * ROWS, ROWS, 0)
    unit_x, inv_x = normalize(own_images)
    unit_y, inv_y = normalize(texts)
    gx = (gx - unit_y.astype(BF).astype(F32)) * scale
    gy = (gy - unit_x.astype(BF).astype(F32)) * scale
    return unnormalize(unit_x, inv_x, gx), unnormalize(unit_y, inv_y, gy)


def solution(mesh):
    fine = Mesh(mesh.devices.reshape(SIZES), NAMES)
    blk, grp = NAMES[:3], NAMES[3:]
    return jax.shard_map(
        local,
        mesh=fine,
        in_specs=(P(blk, None), P(blk + grp, None), P(), P()),
        out_specs=(P(blk + grp, None), P(blk + grp, None)),
        check_vma=False,
    )
```

```python
import jax
import jax.numpy as jnp
from jax import lax
from jax.sharding import Mesh, PartitionSpec as P

SIZES = (4, 4, 2, 2, 3, 2, 2)
NAMES = ("yl", "x", "c", "yh", "z3", "z2", "z1")
ROWS = 24
BF = jnp.bfloat16
F32 = jnp.float32


def normalize(vectors):
    values = vectors.astype(F32)
    inverse = lax.rsqrt(jnp.sum(values * values, axis=1, keepdims=True) + 1e-06)
    return values * inverse, inverse


def unnormalize(unit_rows, inverse, grad_rows):
    inner = jnp.sum(unit_rows * grad_rows, axis=1, keepdims=True)
    return inverse * (grad_rows - unit_rows * inner)


def pair_perm(size, distance):
    perm = []
    for core in range(2):
        for at in range(size):
            step = distance if (at // distance) % 2 == 0 else -distance
            if core:
                step = -step
            perm.append((core * size + at, core * size + (at + step) % size))
    return perm


def flip(value, axis, distance):
    size = lax.axis_size(axis)
    return lax.ppermute(value, axis, [(i, i ^ distance) for i in range(size)])


def pick(value, axis, index):
    return lax.dynamic_index_in_dim(value, index, axis, keepdims=False)


PLANE = ("yl", "x", "c", "yh")


def member(core, window, pos, x):
    y = (4 * window + pos - 2 * core) % 8
    return ((y % 4 * 4 + x) * 2 + core) * 2 + y // 4


PLACES = [(c, w, p, x) for c in range(2) for w in range(2) for p in range(4) for x in range(4)]


def gather(texts):
    groups = [
        [member(c, w, p, x) for x in range(4) for p in range(4)] for c in range(2) for w in range(2)
    ]
    copies = jnp.broadcast_to(texts[None], (16, *texts.shape))
    own = lax.all_to_all(copies, PLANE, 0, 0, axis_index_groups=groups)
    return own.reshape(-1, texts.shape[1])


def scatter_sum(total):
    pos = (lax.axis_index("yl") + 2 * lax.axis_index("c")) % 4
    for at, dp, dx in ((lax.axis_index("x"), 0, 1), (pos, 1, 0)):
        got = [
            lax.ppermute(
                pick(total, 0, at ^ d).astype(BF),
                PLANE,
                [(member(*m), member(m[0], m[1], m[2] ^ d * dp, m[3] ^ d * dx)) for m in PLACES],
            )
            for d in (1, 2, 3)
        ]
        total = pick(total, 0, at).astype(F32) + got[0].astype(F32) + got[1].astype(F32) + got[2].astype(F32)
    return total


def local(images, texts, log_scale, bias):
    width = texts.shape[1]
    scale = jnp.exp(log_scale[0])
    z1 = lax.axis_index("z1")
    group = lax.axis_index(("yh", "z3", "z2", "z1"))
    blocks = images.reshape(6, 2, 2, ROWS, width)
    mine, theirs = (pick(blocks, 2, i).swapaxes(0, 1).reshape(12, ROWS, width) for i in (z1, 1 - z1))
    image_rows = jnp.concatenate([theirs, mine], 0).reshape(-1, width)
    own = gather(texts)
    other = flip(own, "c", 1)
    text_rows = jnp.concatenate([own, other], 0)
    xn = normalize(image_rows)[0].astype(BF)
    yn = lax.optimization_barrier(normalize(text_rows)[0].astype(BF))
    logits = jnp.dot(xn, yn.T, preferred_element_type=F32) * scale + bias[0]
    w = jax.nn.sigmoid(logits).astype(BF)
    half = xn.shape[0] // 2
    n_own = own.shape[0]
    gx_send = jnp.dot(w[:half], yn, preferred_element_type=F32).astype(BF)
    w, gx_send = lax.optimization_barrier((w, gx_send))
    gx_got = lax.ppermute(gx_send, ("c", "z3", "z2", "z1"), pair_perm(12, 1))
    gy_other = jnp.einsum("ic,ie->ce", w[:, n_own:], xn, preferred_element_type=F32).astype(BF)
    gy_own = jnp.einsum("ic,ie->ce", w[:, :n_own], xn, preferred_element_type=F32)
    gy_got = flip(gy_other, "c", 1)
    gx_keep = jnp.dot(w[half:], yn, preferred_element_type=F32)
    gx_got, gx_keep = lax.optimization_barrier((gx_got, gx_keep))
    z2 = lax.axis_index("z2")
    gx = (gx_keep + gx_got.astype(F32)).reshape(2, 6, ROWS, width)
    gx_got = lax.ppermute(pick(gx, 0, 1 - z2).astype(BF), ("c", "z3", "z2", "z1"), pair_perm(12, 2))
    gx = (pick(gx, 0, z2) + gx_got.astype(F32)).astype(BF)
    gx = lax.all_to_all(gx, ("yh", "z3"), 0, 0)
    gy = (gy_own + gy_got.astype(F32)).astype(BF).reshape(4, 4, ROWS, width)
    gy = scatter_sum(gy)
    gx = jnp.sum(gx.astype(F32), 0)
    own_images = lax.optimization_barrier(lax.dynamic_slice_in_dim(images, group * ROWS, ROWS, 0))
    unit_x, inv_x = normalize(own_images)
    unit_y, inv_y = normalize(texts)
    gx = (gx - unit_y.astype(BF).astype(F32)) * scale
    gy = (gy - unit_x.astype(BF).astype(F32)) * scale
    return unnormalize(unit_x, inv_x, gx), unnormalize(unit_y, inv_y, gy)


def solution(mesh):
    fine = Mesh(mesh.devices.reshape(SIZES), NAMES)
    blk, grp = NAMES[:3], NAMES[3:]
    return jax.shard_map(
        local,
        mesh=fine,
        in_specs=(P(blk, None), P(blk + grp, None), P(), P()),
        out_specs=(P(blk + grp, None), P(blk + grp, None)),
        check_vma=False,
    )
```

```python
import jax
import jax.numpy as jnp
from jax import lax
from jax.sharding import Mesh, PartitionSpec as P

SIZES = (4, 4, 2, 2, 3, 2, 2)
NAMES = ("yl", "x", "c", "yh", "z3", "z2", "z1")
ROWS = 24
BF = jnp.bfloat16
F32 = jnp.float32


def normalize(vectors):
    values = vectors.astype(F32)
    inverse = lax.rsqrt(jnp.sum(values * values, axis=1, keepdims=True) + 1e-06)
    return values * inverse, inverse


def unnormalize(unit_rows, inverse, grad_rows):
    inner = jnp.sum(unit_rows * grad_rows, axis=1, keepdims=True)
    return inverse * (grad_rows - unit_rows * inner)


def pair_perm(size, distance):
    perm = []
    for core in range(2):
        for at in range(size):
            step = distance if (at // distance) % 2 == 0 else -distance
            if core:
                step = -step
            perm.append((core * size + at, core * size + (at + step) % size))
    return perm


def flip(value, axis, distance):
    size = lax.axis_size(axis)
    return lax.ppermute(value, axis, [(i, i ^ distance) for i in range(size)])


def pick(value, axis, index):
    return lax.dynamic_index_in_dim(value, index, axis, keepdims=False)


PLANE = ("yl", "x", "c", "yh")


def member(core, window, pos, x):
    y = (4 * window + pos - 2 * core) % 8
    return ((y % 4 * 4 + x) * 2 + core) * 2 + y // 4


PLACES = [(c, w, p, x) for c in range(2) for w in range(2) for p in range(4) for x in range(4)]


def gather(texts):
    groups = [
        [member(c, w, p, x) for x in range(4) for p in range(4)] for c in range(2) for w in range(2)
    ]
    copies = jnp.broadcast_to(texts[None], (16, *texts.shape))
    own = lax.all_to_all(copies, PLANE, 0, 0, axis_index_groups=groups)
    return own.reshape(-1, texts.shape[1])


def scatter_sum(total):
    pos = (lax.axis_index("yl") + 2 * lax.axis_index("c")) % 4
    for at, dp, dx in ((lax.axis_index("x"), 0, 1), (pos, 1, 0)):
        got = [
            lax.ppermute(
                pick(total, 0, at ^ d).astype(BF),
                PLANE,
                [(member(*m), member(m[0], m[1], m[2] ^ d * dp, m[3] ^ d * dx)) for m in PLACES],
            )
            for d in (1, 2, 3)
        ]
        total = pick(total, 0, at) + got[0].astype(F32) + got[1].astype(F32) + got[2].astype(F32)
    return total


def local(images, texts, log_scale, bias):
    width = texts.shape[1]
    scale = jnp.exp(log_scale[0])
    z1 = lax.axis_index("z1")
    group = lax.axis_index(("yh", "z3", "z2", "z1"))
    blocks = images.reshape(6, 2, 2, ROWS, width)
    mine, theirs = (pick(blocks, 2, i).swapaxes(0, 1).reshape(12, ROWS, width) for i in (z1, 1 - z1))
    image_rows = jnp.concatenate([theirs, mine], 0).reshape(-1, width)
    own = gather(texts)
    other = flip(own, "c", 1)
    text_rows = jnp.concatenate([own, other], 0)
    xn = normalize(image_rows)[0].astype(BF)
    yn = lax.optimization_barrier(normalize(text_rows)[0].astype(BF))
    logits = jnp.dot(xn, yn.T, preferred_element_type=F32) * scale + bias[0]
    w = jax.nn.sigmoid(logits).astype(BF)
    half = xn.shape[0] // 2
    n_own = own.shape[0]
    gx_send = jnp.dot(w[:half], yn, preferred_element_type=F32).astype(BF)
    w, gx_send = lax.optimization_barrier((w, gx_send))
    gx_got = lax.ppermute(gx_send, ("c", "z3", "z2", "z1"), pair_perm(12, 1))
    gy_other = jnp.einsum("ic,ie->ce", w[:, n_own:], xn, preferred_element_type=F32).astype(BF)
    gy_own = jnp.einsum("ic,ie->ce", w[:, :n_own], xn, preferred_element_type=F32)
    gy_got = flip(gy_other, "c", 1)
    gx_keep = jnp.dot(w[half:], yn, preferred_element_type=F32)
    gx_got, gx_keep = lax.optimization_barrier((gx_got, gx_keep))
    z2 = lax.axis_index("z2")
    gx = (gx_keep + gx_got.astype(F32)).reshape(2, 6, ROWS, width)
    gx_got = lax.ppermute(pick(gx, 0, 1 - z2).astype(BF), ("c", "z3", "z2", "z1"), pair_perm(12, 2))
    gx = (pick(gx, 0, z2) + gx_got.astype(F32)).astype(BF)
    gx = lax.all_to_all(gx, ("yh", "z3"), 0, 0)
    gy = (gy_own + gy_got.astype(F32)).reshape(4, 4, ROWS, width)
    gy = scatter_sum(gy)
    gx = jnp.sum(gx.astype(F32), 0)
    own_images = lax.optimization_barrier(lax.dynamic_slice_in_dim(images, group * ROWS, ROWS, 0))
    unit_x, inv_x = normalize(own_images)
    unit_y, inv_y = normalize(texts)
    gx = (gx - unit_y.astype(BF).astype(F32)) * scale
    gy = (gy - unit_x.astype(BF).astype(F32)) * scale
    return unnormalize(unit_x, inv_x, gx), unnormalize(unit_y, inv_y, gy)


def solution(mesh):
    fine = Mesh(mesh.devices.reshape(SIZES), NAMES)
    blk, grp = NAMES[:3], NAMES[3:]
    return jax.shard_map(
        local,
        mesh=fine,
        in_specs=(P(blk, None), P(blk + grp, None), P(), P()),
        out_specs=(P(blk + grp, None), P(blk + grp, None)),
        check_vma=False,
    )
```
